32 devices in a mesh: tensor: 16 (over z, y, x), replica: 2 (over core).
Axes of the slice: x: 2, y: 2, z: 4, core: 2. Of those that a mesh axis runs over, the one named last changes fastest.
Arguments:
- amplitudes: bfloat16 [256, 64, 128], P('tensor'), may hold values from -6 to 6
- block_slot: int32 [256], replicated, may hold values from 0 to 255, each once
- integrals: bfloat16 [256, 16, 64, 64], P('tensor', 'replica'), may hold values from -0.1875 to 0.1875
- tile_cols: int32 [256, 16], P('tensor'), may hold values from 0 to 255, as said below
- irreps: int32 [256], replicated, may hold values from 0 to 7, as said below
Outputs:
- ladder: float32 [256, 64, 128], P('tensor', None, 'replica')
The draws below stay inside these ranges and needn't reach their ends.
Inputs may be any that keep to these rules, and one draw needn't show every extreme that they name: `block_slot`: each block has one slot and each slot one block. `tile_cols`: the tiles of a row that name blocks of the row's own irrep name distinct blocks; other tiles may name any block of another irrep. `irreps`: each irrep labels exactly 32 blocks.
All inputs are finite; a program needn't handle non-finite values.
Results may differ from the reference program's by a relative error of at most 0.0003.
Values may be sent and summed in bfloat16 or wider, within the bound.
A program may use at most 128 MiB of HBM per device.

```python
import jax
import jax.numpy as jnp
from jax import lax

TILE = 64
OCCP = 128
NIRR = 8
NBLK = 256
NZ_ROW = 16


def symmetry_labels(key):
    shuffled = jax.random.permutation(jax.random.fold_in(key, 11), NBLK).astype(jnp.int32)
    labels = (shuffled % NIRR).astype(jnp.int32)
    members = jnp.zeros((NBLK,), jnp.int32).at[shuffled].set(jnp.arange(NBLK, dtype=jnp.int32))
    return (labels, members)


def draw_irreps(key, part):
    labels, members = symmetry_labels(key)
    return labels


def draw_tile_cols(key, part):
    labels, members = symmetry_labels(key)
    per_irrep = NBLK // NIRR
    scores = jax.random.randint(jax.random.fold_in(key, 21), (NBLK, per_irrep), 0, 1 << 20).astype(jnp.int32)
    scores = scores * per_irrep + jnp.arange(per_irrep, dtype=jnp.int32)[None, :]
    ranks = jnp.argsort(scores, axis=1)[:, :NZ_ROW].astype(jnp.int32)
    own_cols = members[labels[:, None] + NIRR * ranks]
    flipped = jax.random.randint(jax.random.fold_in(key, 31), (NBLK, NZ_ROW), 0, 8) == 0
    offset = jax.random.randint(jax.random.fold_in(key, 41), (NBLK, NZ_ROW), 1, NIRR).astype(jnp.int32)
    other_irrep = (labels[:, None] + offset) % NIRR
    other_rank = jax.random.randint(jax.random.fold_in(key, 51), (NBLK, NZ_ROW), 0, per_irrep).astype(jnp.int32)
    other_cols = members[other_irrep + NIRR * other_rank]
    return jnp.where(flipped, other_cols, own_cols).astype(jnp.int32)


def level_of(rng, dims, pieces, low, largest):
    level = 1.0
    for dim, shards_of in pieces:
        draws = jax.random.uniform(jax.random.fold_in(jax.random.fold_in(rng, 6), dim), (shards_of,), jnp.float32, low / len(pieces), largest / len(pieces))
        level = level * jnp.repeat(jnp.exp(draws), dims[dim] // shards_of).reshape((-1,) + (1,) * (len(dims) - 1 - dim))
    return level


def bell_draw(own_key, shape, spread, reach, split=(), held_as=jnp.bfloat16):
    result = jax.random.normal(own_key, shape, jnp.float32) * spread
    if len(split) > 0:
        result = level_of(own_key, shape, split, -0.22, 0.18) * result
    return jnp.clip(result, min=-reach, max=reach).astype(held_as)


def setup_inputs(seed: int = 0) -> dict:
    keys = jax.random.split(jax.random.key(seed), 6)
    amplitudes = bell_draw(keys[0], (NBLK, TILE, OCCP), 1.0, 6.0, ((0, 16),))
    block_slot = jax.random.permutation(keys[1], NBLK).astype(jnp.int32)
    integrals = bell_draw(keys[2], (NBLK, NZ_ROW, TILE, TILE), (TILE * NZ_ROW) ** -0.5, 0.1875, ((0, 16), (1, 2)))
    tile_cols = draw_tile_cols(jax.random.fold_in(keys[5], 71), 0)
    irreps = draw_irreps(jax.random.fold_in(keys[5], 71), 0)
    return {"amplitudes": amplitudes, "block_slot": block_slot, "integrals": integrals, "tile_cols": tile_cols, "irreps": irreps}


def reference(amplitudes, block_slot, integrals, tile_cols, irreps):
    natural = amplitudes[block_slot]

    def one_row(index):
        cols = tile_cols[index]
        allowed = (irreps[cols] == irreps[index]).astype(jnp.bfloat16)
        tiles = integrals[index] * allowed[:, None, None]
        picked = natural[cols]
        return jnp.einsum("nxy,nyp->xp", tiles.astype(jnp.float32), picked.astype(jnp.float32), precision=lax.Precision.HIGHEST)

    return lax.map(one_row, jnp.arange(NBLK, dtype=jnp.int32))
```

```python
import functools

import jax
import jax.numpy as jnp
from jax import lax
from jax.experimental import pallas as pl
from jax.experimental.pallas import tpu as pltpu
from jax.sharding import PartitionSpec as P

MESH = pl.DeviceIdType.MESH
ORDERS = ("yzx", "xzy")
X, Y, UP, DOWN = range(4)


def kernel(
    tensor, replica,
    slot_ref, cols_ref, irreps_ref, amp_hbm, tiles_hbm, out_ref,
    amps, tiles, lhs, index, outgo, income,
    local_sem, send_sem, recv_sem, pass_sem, got_sem, sum_send, sum_recv,
):
    layers = tensor // 4
    blocks = amp_hbm.shape[0]
    part = blocks // replica
    chunk = part // len(ORDERS)
    rows, per_rep = tiles.shape[0], tiles.shape[1]
    width = out_ref.shape[2]
    groups, wide = lhs.shape[1], per_rep // lhs.shape[1]
    zero_block = tensor * blocks
    t, r = lax.axis_index("tensor"), lax.axis_index("replica")
    z, y, x = t // 4, (t // 2) % 2, t % 2

    own = pltpu.make_async_copy(amp_hbm, amps.at[pl.ds(t * blocks, blocks)], local_sem.at[0])
    own.start()
    load_tiles = pltpu.make_async_copy(tiles_hbm, tiles, local_sem.at[1])
    load_tiles.start()

    target = {X: t + 1 - 2 * x, Y: t + 2 - 4 * y, UP: t + 4, DOWN: t - 4}
    exists = {X: None, Y: None, UP: z < layers - 1, DOWN: z > 0}

    def when(condition, body):
        if condition is None:
            body()
        else:
            pl.when(condition)(body)

    def both(a, b):
        return b if a is None else a if b is None else a & b

    barrier = pltpu.get_barrier_semaphore()

    def greet(device):
        pl.semaphore_signal(barrier, inc=1, device_id=device, device_id_type=MESH)

    for way in (X, Y, UP, DOWN):
        when(exists[way], functools.partial(greet, {"tensor": target[way], "replica": r}))
    for j in range(1, replica):
        greet({"tensor": t, "replica": (r + j) % replica})
    ends = (z == 0).astype(jnp.int32) + (z == layers - 1).astype(jnp.int32)
    pl.semaphore_wait(barrier, 4 - ends + replica - 1)

    def place(source, owner, flow):
        return amps.at[pl.ds(source * blocks + owner * part + flow * chunk, chunk)]

    def hop(flow, source, way):
        return pltpu.make_async_remote_copy(
            src_ref=place(source, r, flow), dst_ref=place(source, r, flow),
            send_sem=send_sem.at[flow, source, way], recv_sem=recv_sem.at[flow, source],
            device_id={"tensor": jnp.clip(target[way], 0, tensor - 1), "replica": r}, device_id_type=MESH,
        )

    def handover(flow, source, j):
        return pltpu.make_async_remote_copy(
            src_ref=place(source, r, flow), dst_ref=place(source, r, flow),
            send_sem=pass_sem.at[j - 1, flow, source], recv_sem=got_sem.at[j - 1, flow, source],
            device_id={"tensor": t, "replica": (r + j) % replica}, device_id_type=MESH,
        )

    def ways(flow, dx, dy, dz):
        order = ORDERS[flow]
        moved = {"x": dx, "y": dy, "z": dz}
        last = max([i for i, axis in enumerate(order) if moved[axis]], default=-1)
        found = []
        if last >= 0 and order[last] == "z":
            found.append(UP if dz > 0 else DOWN)
        for axis in order[last + 1:]:
            found += {"x": [X], "y": [Y], "z": [UP, DOWN]}[axis]
        return found

    def visit(action):
        def ring(k, carry):
            for flow in range(len(ORDERS)):
                for dx, dy in ((0, 0), (1, 0), (0, 1), (1, 1)):
                    d = k - dx - dy
                    base = t + dx * (1 - 2 * x) + dy * (2 - 4 * y)
                    if dx or dy:
                        action(d == 0, flow, base, ways(flow, dx, dy, 0))
                    for dz in (1, -1):
                        inside = (d >= 1) & ((d <= z) if dz > 0 else (d <= layers - 1 - z))
                        action(inside, flow, base - 4 * dz * d, ways(flow, dx, dy, dz))
            return carry

        lax.fori_loop(1, layers + 2, ring, 0)

    own.wait()
    for flow in range(len(ORDERS)):
        for way in ways(flow, 0, 0, 0):
            when(exists[way], lambda flow=flow, way=way: hop(flow, t, way).start())

    amps[zero_block] = jnp.zeros(amps.shape[1:], amps.dtype)
    load_tiles.wait()

    def pack(b, carry):
        for g in range(groups):
            lhs[b, g] = jnp.concatenate([tiles[b, g * wide + i] for i in range(wide)], axis=1)
        for n in range(per_rep):
            col = cols_ref[b, r * per_rep + n]
            same = irreps_ref[col] == irreps_ref[t * rows + b]
            index[b * per_rep + n] = jnp.where(same, slot_ref[col], zero_block)
        return carry

    lax.fori_loop(0, rows, pack, 0)

    def forward(condition, flow, source, onward):
        @pl.when(condition)
        def _():
            hop(flow, source, X).wait_recv()
            for way in onward:
                when(exists[way], lambda way=way: hop(flow, source, way).start())
            for j in range(1, replica):
                handover(flow, source, j).start()

    visit(forward)

    def arrived(condition, flow, source, onward):
        @pl.when(condition)
        def _():
            for j in range(1, replica):
                handover(flow, source, j).wait_recv()

    def got(source, carry):
        @pl.when(source != t)
        def _():
            for flow in range(len(ORDERS)):
                for j in range(1, replica):
                    pltpu.make_async_remote_copy(
                        src_ref=place(source, (r + replica - j) % replica, flow),
                        dst_ref=place(source, (r + replica - j) % replica, flow),
                        send_sem=pass_sem.at[j - 1, flow, source], recv_sem=got_sem.at[j - 1, flow, source],
                        device_id={"tensor": t, "replica": (r + j) % replica}, device_id_type=MESH,
                    ).wait_recv()
        return carry

    lax.fori_loop(0, tensor, got, 0)

    packs = rows // replica

    def sums(q, j):
        return pltpu.make_async_remote_copy(
            src_ref=outgo.at[j, q], dst_ref=income.at[j - 1, q],
            send_sem=sum_send.at[j - 1, q], recv_sem=sum_recv.at[j - 1, q],
            device_id={"tensor": t, "replica": (r + j) % replica}, device_id_type=MESH,
        )

    for q in range(packs):
        turned = []
        for i in range(replica):
            b = q * replica + i
            total = None
            for g in range(groups):
                rhs = jnp.concatenate(
                    [amps[index[b * per_rep + g * wide + n]] for n in range(wide)], axis=0
                )
                term = jnp.dot(lhs[b, g], rhs, preferred_element_type=jnp.float32)
                total = term if total is None else total + term
            turned.append(pltpu.roll(total, (replica - r) % replica * width, 1))
        for j in range(replica):
            outgo[j, q] = jnp.concatenate([v[:, j * width:(j + 1) * width] for v in turned], axis=1)
        for j in range(1, replica):
            sums(q, j).start()

    for q in range(packs):
        total = outgo[0, q]
        for j in range(1, replica):
            sums(q, j).wait_recv()
            total = total + income[j - 1, q]
        for i in range(replica):
            out_ref[q * replica + i] = total[:, i * width:(i + 1) * width]

    for flow in range(len(ORDERS)):
        for way in ways(flow, 0, 0, 0):
            when(exists[way], lambda flow=flow, way=way: hop(flow, t, way).wait_send())

    def sent(condition, flow, source, onward):
        @pl.when(condition)
        def _():
            for way in onward:
                when(exists[way], lambda way=way: hop(flow, source, way).wait_send())
            for j in range(1, replica):
                handover(flow, source, j).wait_send()

    visit(sent)
    for q in range(packs):
        for j in range(1, replica):
            sums(q, j).wait_send()


def solution(mesh):
    tensor, replica = mesh.shape["tensor"], mesh.shape["replica"]

    def local(amplitudes, block_slot, integrals, tile_cols, irreps):
        blocks, tile, occ = amplitudes.shape
        rows, per_rep = integrals.shape[:2]
        wide = max(w for w in (4, 2, 1) if per_rep % w == 0)
        groups = per_rep // wide
        packs = rows // replica
        flows = len(ORDERS)
        smem = pl.BlockSpec(memory_space=pltpu.SMEM)
        hbm = pl.BlockSpec(memory_space=pl.ANY)
        dma = pltpu.SemaphoreType.DMA
        others = max(replica - 1, 1)
        return pl.pallas_call(
            functools.partial(kernel, tensor, replica),
            out_shape=jax.ShapeDtypeStruct((rows, tile, occ // replica), jnp.float32),
            in_specs=[smem, smem, smem, hbm, hbm],
            out_specs=pl.BlockSpec(memory_space=pltpu.VMEM),
            scratch_shapes=[
                pltpu.VMEM((tensor * blocks + 1, tile, occ), amplitudes.dtype),
                pltpu.VMEM(integrals.shape, integrals.dtype),
                pltpu.VMEM((rows, groups, tile, wide * tile), integrals.dtype),
                pltpu.SMEM((rows * per_rep,), jnp.int32),
                pltpu.VMEM((replica, packs, tile, occ), jnp.float32),
                pltpu.VMEM((others, packs, tile, occ), jnp.float32),
                dma((2,)),
                dma((flows, tensor, 4)),
                dma((flows, tensor)),
                dma((others, flows, tensor)),
                dma((others, flows, tensor)),
                dma((others, packs)),
                dma((others, packs)),
            ],
            compiler_params=pltpu.CompilerParams(
                collective_id=0, has_side_effects=True, vmem_limit_bytes=48 << 20
            ),
            cost_estimate=pl.CostEstimate(
                flops=2 * rows * per_rep * tile * tile * occ, bytes_accessed=4 << 20, transcendentals=0
            ),
        )(block_slot, tile_cols, irreps, amplitudes, integrals)

    in_specs = (
        P("tensor", None, None),
        P(),
        P("tensor", "replica", None, None),
        P("tensor", None),
        P(),
    )
    out_specs = P("tensor", None, "replica")
    return jax.shard_map(local, mesh=mesh, in_specs=in_specs, out_specs=out_specs, check_vma=False)
```

```python
import functools

import jax
import jax.numpy as jnp
from jax import lax
from jax.experimental import pallas as pl
from jax.experimental.pallas import tpu as pltpu
from jax.sharding import PartitionSpec as P

MESH = pl.DeviceIdType.MESH
X, Y, UP, DOWN = range(4)


def split(part):
    plan = (("zyx", 1), ("zxy", 1))
    total = sum(n for _, n in plan)
    if part % total:
        plan, total = (("yzx", 1), ("xzy", 1)), 2
    if part % total:
        plan, total = (("yzx", 1),), 1
    flows, first = [], 0
    for order, n in plan:
        flows.append((order, first, n * part // total))
        first += n * part // total
    return flows


def kernel(
    tensor, replica,
    slot_hbm, cols_hbm, irreps_hbm, amp_hbm, tiles_hbm, out_ref,
    amps, tiles, lhs, index, slot_ref, cols_ref, irreps_ref, outgo, income,
    local_sem, send_sem, recv_sem, pass_sem, got_sem, sum_send, sum_recv,
):
    layers = tensor // 4
    blocks = amp_hbm.shape[0]
    part = blocks // replica
    flows = split(part)
    rows, per_rep = tiles.shape[0], tiles.shape[1]
    width = out_ref.shape[2]
    groups, wide = lhs.shape[1], per_rep // lhs.shape[1]
    zero_block = tensor * blocks
    t, r = lax.axis_index("tensor"), lax.axis_index("replica")
    z, y, x = t // 4, (t // 2) % 2, t % 2

    own = pltpu.make_async_copy(amp_hbm, amps.at[pl.ds(t * blocks, blocks)], local_sem.at[0])
    own.start()
    load_tiles = pltpu.make_async_copy(tiles_hbm, tiles, local_sem.at[1])
    load_tiles.start()
    small = [
        pltpu.make_async_copy(src, dst, local_sem.at[2 + i])
        for i, (src, dst) in enumerate(((slot_hbm, slot_ref), (cols_hbm, cols_ref), (irreps_hbm, irreps_ref)))
    ]
    for copy in small:
        copy.start()

    target = {X: t + 1 - 2 * x, Y: t + 2 - 4 * y, UP: t + 4, DOWN: t - 4}
    exists = {X: None, Y: None, UP: z < layers - 1, DOWN: z > 0}

    def when(condition, body):
        if condition is None:
            body()
        else:
            pl.when(condition)(body)

    def both(a, b):
        return b if a is None else a if b is None else a & b

    barrier = pltpu.get_barrier_semaphore()

    def greet(device):
        pl.semaphore_signal(barrier, inc=1, device_id=device, device_id_type=MESH)

    for way in (X, Y, UP, DOWN):
        when(exists[way], functools.partial(greet, {"tensor": target[way], "replica": r}))
    for j in range(1, replica):
        greet({"tensor": t, "replica": (r + j) % replica})
    ends = (z == 0).astype(jnp.int32) + (z == layers - 1).astype(jnp.int32)
    pl.semaphore_wait(barrier, 4 - ends + replica - 1)

    def place(source, owner, flow):
        return amps.at[pl.ds(source * blocks + owner * part + flows[flow][1], flows[flow][2])]

    def hop(flow, source, way):
        return pltpu.make_async_remote_copy(
            src_ref=place(source, r, flow), dst_ref=place(source, r, flow),
            send_sem=send_sem.at[flow, source, way], recv_sem=recv_sem.at[flow, source],
            device_id={"tensor": jnp.clip(target[way], 0, tensor - 1), "replica": r}, device_id_type=MESH,
        )

    def handover(flow, source, j):
        return pltpu.make_async_remote_copy(
            src_ref=place(source, r, flow), dst_ref=place(source, r, flow),
            send_sem=pass_sem.at[j - 1, flow, source], recv_sem=got_sem.at[j - 1, flow, source],
            device_id={"tensor": t, "replica": (r + j) % replica}, device_id_type=MESH,
        )

    def ways(flow, dx, dy, dz):
        order = flows[flow][0]
        moved = {"x": dx, "y": dy, "z": dz}
        last = max([i for i, axis in enumerate(order) if moved[axis]], default=-1)
        found = []
        if last >= 0 and order[last] == "z":
            found.append(UP if dz > 0 else DOWN)
        for axis in order[last + 1:]:
            found += {"x": [X], "y": [Y], "z": [UP, DOWN]}[axis]
        return found

    def visit(action):
        def ring(k, carry):
            for flow in range(len(flows)):
                for dx, dy in ((0, 0), (1, 0), (0, 1), (1, 1)):
                    d = k - dx - dy
                    base = t + dx * (1 - 2 * x) + dy * (2 - 4 * y)
                    if dx or dy:
                        action(d == 0, flow, base, ways(flow, dx, dy, 0))
                    for dz in (1, -1):
                        inside = (d >= 1) & ((d <= z) if dz > 0 else (d <= layers - 1 - z))
                        action(inside, flow, base - 4 * dz * d, ways(flow, dx, dy, dz))
            return carry

        lax.fori_loop(1, layers + 2, ring, 0)

    own.wait()
    for flow in range(len(flows)):
        for way in ways(flow, 0, 0, 0):
            when(exists[way], lambda flow=flow, way=way: hop(flow, t, way).start())

    amps[zero_block] = jnp.zeros(amps.shape[1:], amps.dtype)
    load_tiles.wait()
    for copy in small:
        copy.wait()

    def pack(b, carry):
        for g in range(groups):
            lhs[b, g] = jnp.concatenate([tiles[b, g * wide + i] for i in range(wide)], axis=1)
        for n in range(per_rep):
            col = cols_ref[b, r * per_rep + n]
            same = irreps_ref[col] == irreps_ref[t * rows + b]
            index[b * per_rep + n] = jnp.where(same, slot_ref[col], zero_block)
        return carry

    lax.fori_loop(0, rows, pack, 0)

    def forward(condition, flow, source, onward):
        @pl.when(condition)
        def _():
            hop(flow, source, X).wait_recv()
            for way in onward:
                when(exists[way], lambda way=way: hop(flow, source, way).start())
            for j in range(1, replica):
                handover(flow, source, j).start()

    visit(forward)

    def got(source, carry):
        @pl.when(source != t)
        def _():
            for flow in range(len(flows)):
                for j in range(1, replica):
                    pltpu.make_async_remote_copy(
                        src_ref=place(source, (r + replica - j) % replica, flow),
                        dst_ref=place(source, (r + replica - j) % replica, flow),
                        send_sem=pass_sem.at[j - 1, flow, source], recv_sem=got_sem.at[j - 1, flow, source],
                        device_id={"tensor": t, "replica": (r + j) % replica}, device_id_type=MESH,
                    ).wait_recv()
        return carry

    lax.fori_loop(0, tensor, got, 0)

    packs = rows // replica

    def sums(q, j):
        return pltpu.make_async_remote_copy(
            src_ref=outgo.at[j, q], dst_ref=income.at[j - 1, q],
            send_sem=sum_send.at[j - 1, q], recv_sem=sum_recv.at[j - 1, q],
            device_id={"tensor": t, "replica": (r + j) % replica}, device_id_type=MESH,
        )

    for q in range(packs):
        turned = []
        for i in range(replica):
            b = q * replica + i
            total = None
            for g in range(groups):
                rhs = jnp.concatenate(
                    [amps[index[b * per_rep + g * wide + n]] for n in range(wide)], axis=0
                )
                term = jnp.dot(lhs[b, g], rhs, preferred_element_type=jnp.float32)
                total = term if total is None else total + term
            turned.append(pltpu.roll(total, (replica - r) % replica * width, 1))
        for j in range(replica):
            outgo[j, q] = jnp.concatenate([v[:, j * width:(j + 1) * width] for v in turned], axis=1)
        for j in range(1, replica):
            sums(q, j).start()

    for q in range(packs):
        total = outgo[0, q]
        for j in range(1, replica):
            sums(q, j).wait_recv()
            total = total + income[j - 1, q]
        for i in range(replica):
            out_ref[q * replica + i] = total[:, i * width:(i + 1) * width]

    for flow in range(len(flows)):
        for way in ways(flow, 0, 0, 0):
            when(exists[way], lambda flow=flow, way=way: hop(flow, t, way).wait_send())

    def sent(condition, flow, source, onward):
        @pl.when(condition)
        def _():
            for way in onward:
                when(exists[way], lambda way=way: hop(flow, source, way).wait_send())
            for j in range(1, replica):
                handover(flow, source, j).wait_send()

    visit(sent)
    for q in range(packs):
        for j in range(1, replica):
            sums(q, j).wait_send()


def solution(mesh):
    tensor, replica = mesh.shape["tensor"], mesh.shape["replica"]

    def local(amplitudes, block_slot, integrals, tile_cols, irreps):
        blocks, tile, occ = amplitudes.shape
        rows, per_rep = integrals.shape[:2]
        wide = max(w for w in (4, 2, 1) if per_rep % w == 0)
        groups = per_rep // wide
        packs = rows // replica
        flows = len(split(blocks // replica))
        hbm = pl.BlockSpec(memory_space=pltpu.HBM)
        dma = pltpu.SemaphoreType.DMA
        others = max(replica - 1, 1)
        return pl.pallas_call(
            functools.partial(kernel, tensor, replica),
            out_shape=jax.ShapeDtypeStruct((rows, tile, occ // replica), jnp.float32),
            in_specs=[hbm] * 5,
            out_specs=pl.BlockSpec(memory_space=pltpu.VMEM),
            scratch_shapes=[
                pltpu.VMEM((tensor * blocks + 1, tile, occ), amplitudes.dtype),
                pltpu.VMEM(integrals.shape, integrals.dtype),
                pltpu.VMEM((rows, groups, tile, wide * tile), integrals.dtype),
                pltpu.SMEM((rows * per_rep,), jnp.int32),
                pltpu.SMEM(block_slot.shape, jnp.int32),
                pltpu.SMEM(tile_cols.shape, jnp.int32),
                pltpu.SMEM(irreps.shape, jnp.int32),
                pltpu.VMEM((replica, packs, tile, occ), jnp.float32),
                pltpu.VMEM((others, packs, tile, occ), jnp.float32),
                dma((5,)),
                dma((flows, tensor, 4)),
                dma((flows, tensor)),
                dma((others, flows, tensor)),
                dma((others, flows, tensor)),
                dma((others, packs)),
                dma((others, packs)),
            ],
            compiler_params=pltpu.CompilerParams(
                collective_id=0, has_side_effects=True, vmem_limit_bytes=60 << 20
            ),
            cost_estimate=pl.CostEstimate(
                flops=2 * rows * per_rep * tile * tile * occ, bytes_accessed=4 << 20, transcendentals=0
            ),
        )(block_slot, tile_cols, irreps, amplitudes, integrals)

    in_specs = (
        P("tensor", None, None),
        P(),
        P("tensor", "replica", None, None),
        P("tensor", None),
        P(),
    )
    out_specs = P("tensor", None, "replica")
    return jax.shard_map(local, mesh=mesh, in_specs=in_specs, out_specs=out_specs, check_vma=False)
```

```python
import functools

import jax
import jax.numpy as jnp
from jax import lax
from jax.experimental import pallas as pl
from jax.experimental.pallas import tpu as pltpu
from jax.sharding import PartitionSpec as P

MESH = pl.DeviceIdType.MESH
X, Y, UP, DOWN = range(4)


def split(part):
    plan = (("zyx", 1), ("zxy", 1))
    total = sum(n for _, n in plan)
    if part % total:
        plan, total = (("yzx", 1), ("xzy", 1)), 2
    if part % total:
        plan, total = (("yzx", 1),), 1
    flows, first = [], 0
    for order, n in plan:
        flows.append((order, first, n * part // total))
        first += n * part // total
    return flows


def kernel(
    tensor, replica,
    slot_hbm, cols_hbm, irreps_hbm, amp_hbm, tiles_hbm, out_ref,
    amps, tiles, lhs, index, slot_ref, cols_ref, irreps_ref, outgo, income,
    local_sem, send_sem, recv_sem, pass_sem, got_sem, sum_send, sum_recv,
):
    layers = tensor // 4
    blocks = amp_hbm.shape[0]
    part = blocks // replica
    flows = split(part)
    rows, per_rep = tiles.shape[0], tiles.shape[1]
    width = out_ref.shape[2]
    groups, wide = lhs.shape[1], per_rep // lhs.shape[1]
    zero_block = tensor * blocks
    t, r = lax.axis_index("tensor"), lax.axis_index("replica")
    z, y, x = t // 4, (t // 2) % 2, t % 2

    own = pltpu.make_async_copy(amp_hbm, amps.at[pl.ds(t * blocks, blocks)], local_sem.at[0])
    own.start()
    load_tiles = pltpu.make_async_copy(tiles_hbm, tiles, local_sem.at[1])
    load_tiles.start()
    small = [
        pltpu.make_async_copy(src, dst, local_sem.at[2 + i])
        for i, (src, dst) in enumerate(((slot_hbm, slot_ref), (cols_hbm, cols_ref), (irreps_hbm, irreps_ref)))
    ]
    for copy in small:
        copy.start()

    target = {X: t + 1 - 2 * x, Y: t + 2 - 4 * y, UP: t + 4, DOWN: t - 4}
    exists = {X: None, Y: None, UP: z < layers - 1, DOWN: z > 0}

    def when(condition, body):
        if condition is None:
            body()
        else:
            pl.when(condition)(body)

    def both(a, b):
        return b if a is None else a if b is None else a & b

    barrier = pltpu.get_barrier_semaphore()

    def greet(device):
        pl.semaphore_signal(barrier, inc=1, device_id=device, device_id_type=MESH)

    for way in (X, Y, UP, DOWN):
        when(exists[way], functools.partial(greet, {"tensor": target[way], "replica": r}))
    for j in range(1, replica):
        greet({"tensor": t, "replica": (r + j) % replica})
    ends = (z == 0).astype(jnp.int32) + (z == layers - 1).astype(jnp.int32)
    pl.semaphore_wait(barrier, 4 - ends + replica - 1)

    def place(source, owner, flow):
        return amps.at[pl.ds(source * blocks + owner * part + flows[flow][1], flows[flow][2])]

    def hop(flow, source, way):
        return pltpu.make_async_remote_copy(
            src_ref=place(source, r, flow), dst_ref=place(source, r, flow),
            send_sem=send_sem.at[flow, source, way], recv_sem=recv_sem.at[flow, source],
            device_id={"tensor": jnp.clip(target[way], 0, tensor - 1), "replica": r}, device_id_type=MESH,
        )

    def handover(flow, source, j):
        return pltpu.make_async_remote_copy(
            src_ref=place(source, r, flow), dst_ref=place(source, r, flow),
            send_sem=pass_sem.at[j - 1, flow, source], recv_sem=got_sem.at[j - 1, flow, source],
            device_id={"tensor": t, "replica": (r + j) % replica}, device_id_type=MESH,
        )

    def ways(flow, dx, dy, dz):
        order = flows[flow][0]
        moved = {"x": dx, "y": dy, "z": dz}
        last = max([i for i, axis in enumerate(order) if moved[axis]], default=-1)
        found = []
        if last >= 0 and order[last] == "z":
            found.append(UP if dz > 0 else DOWN)
        for axis in order[last + 1:]:
            found += {"x": [X], "y": [Y], "z": [UP, DOWN]}[axis]
        return found

    def visit(action):
        def ring(k, carry):
            for dx, dy in ((0, 0), (1, 0), (0, 1), (1, 1)):
                for flow in range(len(flows)):
                    d = k - dx - dy
                    base = t + dx * (1 - 2 * x) + dy * (2 - 4 * y)
                    if dx or dy:
                        action(d == 0, flow, base, ways(flow, dx, dy, 0))
                    for dz in (1, -1):
                        inside = (d >= 1) & ((d <= z) if dz > 0 else (d <= layers - 1 - z))
                        action(inside, flow, base - 4 * dz * d, ways(flow, dx, dy, dz))
            return carry

        lax.fori_loop(1, layers + 2, ring, 0)

    own.wait()
    for flow in range(len(flows)):
        for way in ways(flow, 0, 0, 0):
            when(exists[way], lambda flow=flow, way=way: hop(flow, t, way).start())

    amps[zero_block] = jnp.zeros(amps.shape[1:], amps.dtype)
    load_tiles.wait()
    for copy in small:
        copy.wait()

    def pack(b, carry):
        for g in range(groups):
            lhs[b, g] = jnp.concatenate([tiles[b, g * wide + i] for i in range(wide)], axis=1)
        for n in range(per_rep):
            col = cols_ref[b, r * per_rep + n]
            same = irreps_ref[col] == irreps_ref[t * rows + b]
            index[b * per_rep + n] = jnp.where(same, slot_ref[col], zero_block)
        return carry

    lax.fori_loop(0, rows, pack, 0)

    def forward(condition, flow, source, onward):
        @pl.when(condition)
        def _():
            hop(flow, source, X).wait_recv()
            for way in onward:
                when(exists[way], lambda way=way: hop(flow, source, way).start())
            for j in range(1, replica):
                handover(flow, source, j).start()

    visit(forward)

    def got(source, carry):
        @pl.when(source != t)
        def _():
            for flow in range(len(flows)):
                for j in range(1, replica):
                    pltpu.make_async_remote_copy(
                        src_ref=place(source, (r + replica - j) % replica, flow),
                        dst_ref=place(source, (r + replica - j) % replica, flow),
                        send_sem=pass_sem.at[j - 1, flow, source], recv_sem=got_sem.at[j - 1, flow, source],
                        device_id={"tensor": t, "replica": (r + j) % replica}, device_id_type=MESH,
                    ).wait_recv()
        return carry

    lax.fori_loop(0, tensor, got, 0)

    packs = rows // replica

    def sums(q, j):
        return pltpu.make_async_remote_copy(
            src_ref=outgo.at[j, q], dst_ref=income.at[j - 1, q],
            send_sem=sum_send.at[j - 1, q], recv_sem=sum_recv.at[j - 1, q],
            device_id={"tensor": t, "replica": (r + j) % replica}, device_id_type=MESH,
        )

    for q in range(packs):
        turned = []
        for i in range(replica):
            b = q * replica + i
            total = None
            for g in range(groups):
                rhs = jnp.concatenate(
                    [amps[index[b * per_rep + g * wide + n]] for n in range(wide)], axis=0
                )
                term = jnp.dot(lhs[b, g], rhs, preferred_element_type=jnp.float32)
                total = term if total is None else total + term
            turned.append(pltpu.roll(total, (replica - r) % replica * width, 1))
        for j in range(replica):
            outgo[j, q] = jnp.concatenate([v[:, j * width:(j + 1) * width] for v in turned], axis=1)
        for j in range(1, replica):
            sums(q, j).start()

    for q in range(packs):
        total = outgo[0, q]
        for j in range(1, replica):
            sums(q, j).wait_recv()
            total = total + income[j - 1, q]
        for i in range(replica):
            out_ref[q * replica + i] = total[:, i * width:(i + 1) * width]

    for flow in range(len(flows)):
        for way in ways(flow, 0, 0, 0):
            when(exists[way], lambda flow=flow, way=way: hop(flow, t, way).wait_send())

    def sent(condition, flow, source, onward):
        @pl.when(condition)
        def _():
            for way in onward:
                when(exists[way], lambda way=way: hop(flow, source, way).wait_send())
            for j in range(1, replica):
                handover(flow, source, j).wait_send()

    visit(sent)
    for q in range(packs):
        for j in range(1, replica):
            sums(q, j).wait_send()


def solution(mesh):
    tensor, replica = mesh.shape["tensor"], mesh.shape["replica"]

    def local(amplitudes, block_slot, integrals, tile_cols, irreps):
        blocks, tile, occ = amplitudes.shape
        rows, per_rep = integrals.shape[:2]
        operands = (block_slot, tile_cols, irreps, amplitudes, integrals)
        wide = max(w for w in (4, 2, 1) if per_rep % w == 0)
        groups = per_rep // wide
        packs = rows // replica
        flows = len(split(blocks // replica))
        hbm = pl.BlockSpec(memory_space=pltpu.HBM)
        dma = pltpu.SemaphoreType.DMA
        others = max(replica - 1, 1)
        return pl.pallas_call(
            functools.partial(kernel, tensor, replica),
            out_shape=jax.ShapeDtypeStruct((rows, tile, occ // replica), jnp.float32),
            in_specs=[hbm] * 5,
            out_specs=pl.BlockSpec(memory_space=pltpu.VMEM),
            scratch_shapes=[
                pltpu.VMEM((tensor * blocks + 1, tile, occ), amplitudes.dtype),
                pltpu.VMEM(integrals.shape, integrals.dtype),
                pltpu.VMEM((rows, groups, tile, wide * tile), integrals.dtype),
                pltpu.SMEM((rows * per_rep,), jnp.int32),
                pltpu.SMEM(block_slot.shape, jnp.int32),
                pltpu.SMEM(tile_cols.shape, jnp.int32),
                pltpu.SMEM(irreps.shape, jnp.int32),
                pltpu.VMEM((replica, packs, tile, occ), jnp.float32),
                pltpu.VMEM((others, packs, tile, occ), jnp.float32),
                dma((5,)),
                dma((flows, tensor, 4)),
                dma((flows, tensor)),
                dma((others, flows, tensor)),
                dma((others, flows, tensor)),
                dma((others, packs)),
                dma((others, packs)),
            ],
            compiler_params=pltpu.CompilerParams(
                collective_id=0, has_side_effects=True, vmem_limit_bytes=48 << 20
            ),
            cost_estimate=pl.CostEstimate(
                flops=2 * rows * per_rep * tile * tile * occ, bytes_accessed=4 << 20, transcendentals=0
            ),
        )(*(pltpu.with_memory_space_constraint(v, pltpu.HBM) for v in operands))

    in_specs = (
        P("tensor", None, None),
        P(),
        P("tensor", "replica", None, None),
        P("tensor", None),
        P(),
    )
    out_specs = P("tensor", None, "replica")
    return jax.shard_map(local, mesh=mesh, in_specs=in_specs, out_specs=out_specs, check_vma=False)
```

```python
import functools

import jax
import jax.numpy as jnp
from jax import lax
from jax.experimental import pallas as pl
from jax.experimental.pallas import tpu as pltpu
from jax.sharding import PartitionSpec as P

MESH = pl.DeviceIdType.MESH
X, Y, UP, DOWN = range(4)


def split(part):
    plan = (("zyx", 1), ("zxy", 1))
    total = sum(n for _, n in plan)
    if part % total:
        plan, total = (("yzx", 1), ("xzy", 1)), 2
    if part % total:
        plan, total = (("yzx", 1),), 1
    flows, first = [], 0
    for order, n in plan:
        flows.append((order, first, n * part // total))
        first += n * part // total
    return flows


def kernel(
    tensor, replica,
    slot_hbm, cols_hbm, irreps_hbm, amp_hbm, tiles_hbm, out_ref,
    amps, tiles, lhs, index, slot_ref, cols_ref, irreps_ref,
    local_sem, send_sem, recv_sem, pass_sem, got_sem, tiles_send, tiles_recv,
):
    layers = tensor // 4
    blocks = amp_hbm.shape[0]
    part = blocks // replica
    flows = split(part)
    rows, per_rep = tiles.shape[0], tiles.shape[1]
    width = out_ref.shape[2]
    groups, wide = lhs.shape[2], per_rep // lhs.shape[2]
    per_row = per_rep * replica
    zero_block = tensor * blocks
    t, r = lax.axis_index("tensor"), lax.axis_index("replica")
    z, y, x = t // 4, (t // 2) % 2, t % 2

    own = pltpu.make_async_copy(amp_hbm, amps.at[pl.ds(t * blocks, blocks)], local_sem.at[0])
    own.start()
    load_tiles = pltpu.make_async_copy(tiles_hbm, tiles, local_sem.at[1])
    load_tiles.start()
    small = [
        pltpu.make_async_copy(src, dst, local_sem.at[2 + i])
        for i, (src, dst) in enumerate(((slot_hbm, slot_ref), (cols_hbm, cols_ref), (irreps_hbm, irreps_ref)))
    ]
    for copy in small:
        copy.start()

    target = {X: t + 1 - 2 * x, Y: t + 2 - 4 * y, UP: t + 4, DOWN: t - 4}
    exists = {X: None, Y: None, UP: z < layers - 1, DOWN: z > 0}

    def when(condition, body):
        if condition is None:
            body()
        else:
            pl.when(condition)(body)

    def both(a, b):
        return b if a is None else a if b is None else a & b

    barrier = pltpu.get_barrier_semaphore()

    def greet(device):
        pl.semaphore_signal(barrier, inc=1, device_id=device, device_id_type=MESH)

    for way in (X, Y, UP, DOWN):
        when(exists[way], functools.partial(greet, {"tensor": target[way], "replica": r}))
    for j in range(1, replica):
        greet({"tensor": t, "replica": (r + j) % replica})
    ends = (z == 0).astype(jnp.int32) + (z == layers - 1).astype(jnp.int32)
    pl.semaphore_wait(barrier, 4 - ends + replica - 1)

    def place(source, owner, flow):
        return amps.at[pl.ds(source * blocks + owner * part + flows[flow][1], flows[flow][2])]

    def hop(flow, source, way):
        return pltpu.make_async_remote_copy(
            src_ref=place(source, r, flow), dst_ref=place(source, r, flow),
            send_sem=send_sem.at[flow, source, way], recv_sem=recv_sem.at[flow, source],
            device_id={"tensor": jnp.clip(target[way], 0, tensor - 1), "replica": r}, device_id_type=MESH,
        )

    def handover(flow, source, j):
        return pltpu.make_async_remote_copy(
            src_ref=place(source, r, flow), dst_ref=place(source, r, flow),
            send_sem=pass_sem.at[j - 1, flow, source], recv_sem=got_sem.at[j - 1, flow, source],
            device_id={"tensor": t, "replica": (r + j) % replica}, device_id_type=MESH,
        )

    def ways(flow, dx, dy, dz):
        order = flows[flow][0]
        moved = {"x": dx, "y": dy, "z": dz}
        last = max([i for i, axis in enumerate(order) if moved[axis]], default=-1)
        found = []
        if last >= 0 and order[last] == "z":
            found.append(UP if dz > 0 else DOWN)
        for axis in order[last + 1:]:
            found += {"x": [X], "y": [Y], "z": [UP, DOWN]}[axis]
        return found

    def visit(action, after=None):
        def ring(k, carry):
            for dx, dy in ((0, 0), (1, 0), (0, 1), (1, 1)):
                for flow in range(len(flows)):
                    d = k - dx - dy
                    base = t + dx * (1 - 2 * x) + dy * (2 - 4 * y)
                    if dx or dy:
                        action(d == 0, flow, base, ways(flow, dx, dy, 0))
                    for dz in (1, -1):
                        inside = (d >= 1) & ((d <= z) if dz > 0 else (d <= layers - 1 - z))
                        action(inside, flow, base - 4 * dz * d, ways(flow, dx, dy, dz))
            if after is not None:
                after(k - 1)
            return carry

        lax.fori_loop(1, layers + 2, ring, 0)

    own.wait()
    for flow in range(len(flows)):
        for way in ways(flow, 0, 0, 0):
            when(exists[way], lambda flow=flow, way=way: hop(flow, t, way).start())

    amps[zero_block] = jnp.zeros(amps.shape[1:], amps.dtype)
    load_tiles.wait()
    for copy in small:
        copy.wait()

    def pack(b, carry):
        for g in range(groups):
            lhs[r, b, g] = jnp.concatenate([tiles[b, g * wide + i] for i in range(wide)], axis=1)
        return carry

    lax.fori_loop(0, rows, pack, 0)

    def share(owner, j):
        return pltpu.make_async_remote_copy(
            src_ref=lhs.at[owner], dst_ref=lhs.at[owner],
            send_sem=tiles_send.at[j - 1], recv_sem=tiles_recv.at[j - 1],
            device_id={"tensor": t, "replica": (r + j) % replica}, device_id_type=MESH,
        )

    for j in range(1, replica):
        share(r, j).start()

    def find(b):
        mine = irreps_ref[t * rows + b]
        for n in range(per_row):
            col = cols_ref[b, n]
            index[b * per_row + n] = jnp.where(irreps_ref[col] == mine, slot_ref[col], zero_block)

    def forward(condition, flow, source, onward):
        @pl.when(condition)
        def _():
            hop(flow, source, X).wait_recv()
            for way in onward:
                when(exists[way], lambda way=way: hop(flow, source, way).start())
            for j in range(1, replica):
                handover(flow, source, j).start()

    share_rows = -(-rows // (layers + 1))

    def find_some(k):
        lax.fori_loop(
            jnp.minimum(k * share_rows, rows), jnp.minimum((k + 1) * share_rows, rows), lambda b, _: (find(b), _)[1], 0
        )

    visit(forward, find_some)

    def got(source, carry):
        @pl.when(source != t)
        def _():
            for flow in range(len(flows)):
                for j in range(1, replica):
                    pltpu.make_async_remote_copy(
                        src_ref=place(source, (r + replica - j) % replica, flow),
                        dst_ref=place(source, (r + replica - j) % replica, flow),
                        send_sem=pass_sem.at[j - 1, flow, source], recv_sem=got_sem.at[j - 1, flow, source],
                        device_id={"tensor": t, "replica": (r + j) % replica}, device_id_type=MESH,
                    ).wait_recv()
        return carry

    lax.fori_loop(0, tensor, got, 0)

    for j in range(1, replica):
        share((r + replica - j) % replica, j).wait_recv()

    for b in range(rows):
        total = None
        for p in range(replica):
            for g in range(groups):
                first = b * per_row + p * per_rep + g * wide
                rhs = jnp.concatenate([amps[index[first + n]] for n in range(wide)], axis=0)
                term = jnp.dot(lhs[p, b, g], rhs, preferred_element_type=jnp.float32)
                total = term if total is None else total + term
        out_ref[b] = pltpu.roll(total, (replica - r) % replica * width, 1)[:, :width]

    for flow in range(len(flows)):
        for way in ways(flow, 0, 0, 0):
            when(exists[way], lambda flow=flow, way=way: hop(flow, t, way).wait_send())

    def sent(condition, flow, source, onward):
        @pl.when(condition)
        def _():
            for way in onward:
                when(exists[way], lambda way=way: hop(flow, source, way).wait_send())
            for j in range(1, replica):
                handover(flow, source, j).wait_send()

    visit(sent)
    for j in range(1, replica):
        share(r, j).wait_send()


def solution(mesh):
    tensor, replica = mesh.shape["tensor"], mesh.shape["replica"]

    def local(amplitudes, block_slot, integrals, tile_cols, irreps):
        blocks, tile, occ = amplitudes.shape
        rows, per_rep = integrals.shape[:2]
        operands = (block_slot, tile_cols, irreps, amplitudes, integrals)
        wide = max(w for w in (4, 2, 1) if per_rep % w == 0)
        groups = per_rep // wide
        flows = len(split(blocks // replica))
        hbm = pl.BlockSpec(memory_space=pltpu.HBM)
        dma = pltpu.SemaphoreType.DMA
        others = max(replica - 1, 1)
        return pl.pallas_call(
            functools.partial(kernel, tensor, replica),
            out_shape=jax.ShapeDtypeStruct((rows, tile, occ // replica), jnp.float32),
            in_specs=[hbm] * 5,
            out_specs=pl.BlockSpec(memory_space=pltpu.VMEM),
            scratch_shapes=[
                pltpu.VMEM((tensor * blocks + 1, tile, occ), amplitudes.dtype),
                pltpu.VMEM(integrals.shape, integrals.dtype),
                pltpu.VMEM((replica, rows, groups, tile, wide * tile), integrals.dtype),
                pltpu.SMEM((rows * per_rep * replica,), jnp.int32),
                pltpu.SMEM(block_slot.shape, jnp.int32),
                pltpu.SMEM(tile_cols.shape, jnp.int32),
                pltpu.SMEM(irreps.shape, jnp.int32),
                dma((5,)),
                dma((flows, tensor, 4)),
                dma((flows, tensor)),
                dma((others, flows, tensor)),
                dma((others, flows, tensor)),
                dma((others,)),
                dma((others,)),
            ],
            compiler_params=pltpu.CompilerParams(
                collective_id=0, has_side_effects=True, vmem_limit_bytes=48 << 20
            ),
            cost_estimate=pl.CostEstimate(
                flops=2 * replica * rows * per_rep * tile * tile * occ, bytes_accessed=4 << 20, transcendentals=0
            ),
        )(*(pltpu.with_memory_space_constraint(v, pltpu.HBM) for v in operands))

    in_specs = (
        P("tensor", None, None),
        P(),
        P("tensor", "replica", None, None),
        P("tensor", None),
        P(),
    )
    out_specs = P("tensor", None, "replica")
    return jax.shard_map(local, mesh=mesh, in_specs=in_specs, out_specs=out_specs, check_vma=False)
```

```python
import functools

import jax
import jax.numpy as jnp
from jax import lax
from jax.experimental import pallas as pl
from jax.experimental.pallas import tpu as pltpu
from jax.sharding import PartitionSpec as P

MESH = pl.DeviceIdType.MESH
X, Y, UP, DOWN = range(4)


def split(part):
    plan = (("zyx", 1), ("xzy", 1))
    total = sum(n for _, n in plan)
    if part % total:
        plan, total = (("yzx", 1), ("xzy", 1)), 2
    if part % total:
        plan, total = (("yzx", 1),), 1
    flows, first = [], 0
    for order, n in plan:
        flows.append((order, first, n * part // total))
        first += n * part // total
    return flows


def kernel(
    tensor, replica,
    slot_hbm, cols_hbm, irreps_hbm, amp_hbm, tiles_hbm, out_ref,
    amps, tiles, lhs, index, slot_ref, cols_ref, irreps_ref,
    local_sem, send_sem, recv_sem, pass_sem, got_sem, tiles_send, tiles_recv,
):
    layers = tensor // 4
    blocks = amp_hbm.shape[0]
    part = blocks // replica
    flows = split(part)
    rows, per_rep = tiles.shape[0], tiles.shape[1]
    width = out_ref.shape[2]
    groups, wide = lhs.shape[2], per_rep // lhs.shape[2]
    per_row = per_rep * replica
    zero_block = tensor * blocks
    t, r = lax.axis_index("tensor"), lax.axis_index("replica")
    z, y, x = t // 4, (t // 2) % 2, t % 2

    own = pltpu.make_async_copy(amp_hbm, amps.at[pl.ds(t * blocks, blocks)], local_sem.at[0])
    own.start()
    load_tiles = pltpu.make_async_copy(tiles_hbm, tiles, local_sem.at[1])
    load_tiles.start()
    small = [
        pltpu.make_async_copy(src, dst, local_sem.at[2 + i])
        for i, (src, dst) in enumerate(((slot_hbm, slot_ref), (cols_hbm, cols_ref), (irreps_hbm, irreps_ref)))
    ]
    for copy in small:
        copy.start()

    target = {X: t + 1 - 2 * x, Y: t + 2 - 4 * y, UP: t + 4, DOWN: t - 4}
    exists = {X: None, Y: None, UP: z < layers - 1, DOWN: z > 0}

    def when(condition, body):
        if condition is None:
            body()
        else:
            pl.when(condition)(body)

    def both(a, b):
        return b if a is None else a if b is None else a & b

    barrier = pltpu.get_barrier_semaphore()

    def greet(device):
        pl.semaphore_signal(barrier, inc=1, device_id=device, device_id_type=MESH)

    for way in (X, Y, UP, DOWN):
        when(exists[way], functools.partial(greet, {"tensor": target[way], "replica": r}))
    for j in range(1, replica):
        greet({"tensor": t, "replica": (r + j) % replica})
    ends = (z == 0).astype(jnp.int32) + (z == layers - 1).astype(jnp.int32)
    pl.semaphore_wait(barrier, 4 - ends + replica - 1)

    def place(source, owner, flow):
        return amps.at[pl.ds(source * blocks + owner * part + flows[flow][1], flows[flow][2])]

    def hop(flow, source, way):
        return pltpu.make_async_remote_copy(
            src_ref=place(source, r, flow), dst_ref=place(source, r, flow),
            send_sem=send_sem.at[flow, source, way], recv_sem=recv_sem.at[flow, source],
            device_id={"tensor": jnp.clip(target[way], 0, tensor - 1), "replica": r}, device_id_type=MESH,
        )

    def handover(source, owner, j):
        share_of = amps.at[pl.ds(source * blocks + owner * part, part)]
        return pltpu.make_async_remote_copy(
            src_ref=share_of, dst_ref=share_of,
            send_sem=pass_sem.at[j - 1, source], recv_sem=got_sem.at[j - 1, source],
            device_id={"tensor": t, "replica": (r + j) % replica}, device_id_type=MESH,
        )

    def ways(flow, dx, dy, dz):
        order = flows[flow][0]
        moved = {"x": dx, "y": dy, "z": dz}
        last = max([i for i, axis in enumerate(order) if moved[axis]], default=-1)
        found = []
        if last >= 0 and order[last] == "z":
            found.append(UP if dz > 0 else DOWN)
        for axis in order[last + 1:]:
            found += {"x": [X], "y": [Y], "z": [UP, DOWN]}[axis]
        return found

    def visit(action, after=None):
        def ring(k, carry):
            for dx, dy in ((0, 0), (1, 0), (0, 1), (1, 1)):
                for flow in range(len(flows)):
                    d = k - dx - dy
                    base = t + dx * (1 - 2 * x) + dy * (2 - 4 * y)
                    if dx or dy:
                        action(d == 0, flow, base, ways(flow, dx, dy, 0))
                    for dz in (1, -1):
                        inside = (d >= 1) & ((d <= z) if dz > 0 else (d <= layers - 1 - z))
                        action(inside, flow, base - 4 * dz * d, ways(flow, dx, dy, dz))
            if after is not None:
                after(k - 1)
            return carry

        lax.fori_loop(1, layers + 2, ring, 0)

    own.wait()
    for flow in range(len(flows)):
        for way in ways(flow, 0, 0, 0):
            when(exists[way], lambda flow=flow, way=way: hop(flow, t, way).start())

    amps[zero_block] = jnp.zeros(amps.shape[1:], amps.dtype)
    load_tiles.wait()
    for copy in small:
        copy.wait()

    def pack(b, carry):
        for g in range(groups):
            lhs[r, b, g] = jnp.concatenate([tiles[b, g * wide + i] for i in range(wide)], axis=1)
        return carry

    lax.fori_loop(0, rows, pack, 0)

    def share(owner, j):
        return pltpu.make_async_remote_copy(
            src_ref=lhs.at[owner], dst_ref=lhs.at[owner],
            send_sem=tiles_send.at[j - 1], recv_sem=tiles_recv.at[j - 1],
            device_id={"tensor": t, "replica": (r + j) % replica}, device_id_type=MESH,
        )

    for j in range(1, replica):
        share(r, j).start()

    def find(b):
        mine = irreps_ref[t * rows + b]
        for n in range(per_row):
            col = cols_ref[b, n]
            index[b * per_row + n] = jnp.where(irreps_ref[col] == mine, slot_ref[col], zero_block)

    def forward(condition, flow, source, onward):
        @pl.when(condition)
        def _():
            hop(flow, source, X).wait_recv()
            for way in onward:
                when(exists[way], lambda way=way: hop(flow, source, way).start())
            if flow == len(flows) - 1:
                for j in range(1, replica):
                    handover(source, r, j).start()

    share_rows = -(-rows // (layers + 1))

    def find_some(k):
        lax.fori_loop(
            jnp.minimum(k * share_rows, rows), jnp.minimum((k + 1) * share_rows, rows), lambda b, _: (find(b), _)[1], 0
        )

    visit(forward, find_some)

    def got(source, carry):
        @pl.when(source != t)
        def _():
            for j in range(1, replica):
                handover(source, (r + replica - j) % replica, j).wait_recv()
        return carry

    lax.fori_loop(0, tensor, got, 0)

    for j in range(1, replica):
        share((r + replica - j) % replica, j).wait_recv()

    for b in range(rows):
        total = None
        for p in range(replica):
            for g in range(groups):
                first = b * per_row + p * per_rep + g * wide
                rhs = jnp.concatenate([amps[index[first + n]] for n in range(wide)], axis=0)
                term = jnp.dot(lhs[p, b, g], rhs, preferred_element_type=jnp.float32)
                total = term if total is None else total + term
        out_ref[b] = pltpu.roll(total, (replica - r) % replica * width, 1)[:, :width]

    for flow in range(len(flows)):
        for way in ways(flow, 0, 0, 0):
            when(exists[way], lambda flow=flow, way=way: hop(flow, t, way).wait_send())

    def sent(condition, flow, source, onward):
        @pl.when(condition)
        def _():
            for way in onward:
                when(exists[way], lambda way=way: hop(flow, source, way).wait_send())
            if flow == len(flows) - 1:
                for j in range(1, replica):
                    handover(source, r, j).wait_send()

    visit(sent)
    for j in range(1, replica):
        share(r, j).wait_send()


def solution(mesh):
    tensor, replica = mesh.shape["tensor"], mesh.shape["replica"]

    def local(amplitudes, block_slot, integrals, tile_cols, irreps):
        blocks, tile, occ = amplitudes.shape
        rows, per_rep = integrals.shape[:2]
        operands = (block_slot, tile_cols, irreps, amplitudes, integrals)
        wide = max(w for w in (4, 2, 1) if per_rep % w == 0)
        groups = per_rep // wide
        flows = len(split(blocks // replica))
        hbm = pl.BlockSpec(memory_space=pltpu.HBM)
        dma = pltpu.SemaphoreType.DMA
        others = max(replica - 1, 1)
        return pl.pallas_call(
            functools.partial(kernel, tensor, replica),
            out_shape=jax.ShapeDtypeStruct((rows, tile, occ // replica), jnp.float32),
            in_specs=[hbm] * 5,
            out_specs=pl.BlockSpec(memory_space=pltpu.VMEM),
            scratch_shapes=[
                pltpu.VMEM((tensor * blocks + 1, tile, occ), amplitudes.dtype),
                pltpu.VMEM(integrals.shape, integrals.dtype),
                pltpu.VMEM((replica, rows, groups, tile, wide * tile), integrals.dtype),
                pltpu.SMEM((rows * per_rep * replica,), jnp.int32),
                pltpu.SMEM(block_slot.shape, jnp.int32),
                pltpu.SMEM(tile_cols.shape, jnp.int32),
                pltpu.SMEM(irreps.shape, jnp.int32),
                dma((5,)),
                dma((flows, tensor, 4)),
                dma((flows, tensor)),
                dma((others, tensor)),
                dma((others, tensor)),
                dma((others,)),
                dma((others,)),
            ],
            compiler_params=pltpu.CompilerParams(
                collective_id=0, has_side_effects=True, vmem_limit_bytes=48 << 20
            ),
            cost_estimate=pl.CostEstimate(
                flops=2 * replica * rows * per_rep * tile * tile * occ, bytes_accessed=4 << 20, transcendentals=0
            ),
        )(*(pltpu.with_memory_space_constraint(v, pltpu.HBM) for v in operands))

    in_specs = (
        P("tensor", None, None),
        P(),
        P("tensor", "replica", None, None),
        P("tensor", None),
        P(),
    )
    out_specs = P("tensor", None, "replica")
    return jax.shard_map(local, mesh=mesh, in_specs=in_specs, out_specs=out_specs, check_vma=False)
```
